32 devices in a mesh: dp: 8 (over y, x, core), mp: 4 (over z).
Axes of the slice: x: 2, y: 2, z: 4, core: 2. Of those that a mesh axis runs over, the one named last changes fastest.
Arguments:
- tokens: bfloat16 [6304, 768], P(('dp', 'mp')), may hold values from -6 to 6
- cotangent: bfloat16 [6304, 768], P(('dp', 'mp')), may hold values from -6 to 6
- ln1_gain: float32 [768], replicated, may hold values from 0.5 to 1.5
- ln1_bias: float32 [768], replicated, may hold values from -3 to 3
- w_query: bfloat16 [768, 768], P('dp', 'mp'), may hold values from -0.21875 to 0.21875
- query_bias: float32 [768], P('mp'), may hold values from -2 to 2
- w_key: bfloat16 [768, 768], P('dp', 'mp'), may hold values from -0.21875 to 0.21875
- w_value: bfloat16 [768, 768], P('dp', 'mp'), may hold values from -0.21875 to 0.21875
- value_bias: float32 [768], P('mp'), may hold values from -2 to 2
- w_out: bfloat16 [768, 768], P('dp', 'mp'), may hold values from -1.75 to 1.75
- out_bias: float32 [768], replicated, may hold values from -2 to 2
- ln2_gain: float32 [768], replicated, may hold values from 0.5 to 1.5
- ln2_bias: float32 [768], replicated, may hold values from -3 to 3
- w_up: bfloat16 [768, 3072], P('dp', 'mp'), may hold values from -0.21875 to 0.21875
- up_bias: float32 [3072], P('mp'), may hold values from -2 to 2
- w_down: bfloat16 [768, 3072], P('dp', 'mp'), may hold values from -0.109375 to 0.109375
- down_bias: float32 [768], replicated, may hold values from -2 to 2
Outputs:
- activations: bfloat16 [6304, 768], P(('dp', 'mp'))
- input_grad: float32 [6304, 768], P(('dp', 'mp'))
- ln1_gain_grad: float32 [768], replicated
- ln1_bias_grad: float32 [768], replicated
- w_query_grad: float32 [768, 768], P('dp', 'mp')
- query_bias_grad: float32 [768], P('mp')
- w_key_grad: float32 [768, 768], P('dp', 'mp')
- w_value_grad: float32 [768, 768], P('dp', 'mp')
- value_bias_grad: float32 [768], P('mp')
- w_out_grad: float32 [768, 768], P('dp', 'mp')
- out_bias_grad: float32 [768], replicated
- ln2_gain_grad: float32 [768], replicated
- ln2_bias_grad: float32 [768], replicated
- w_up_grad: float32 [768, 3072], P('dp', 'mp')
- up_bias_grad: float32 [3072], P('mp')
- w_down_grad: float32 [768, 3072], P('dp', 'mp')
- down_bias_grad: float32 [768], replicated
The draws below stay inside these ranges and needn't reach their ends.
All inputs are finite; a program needn't handle non-finite values.
Results may differ from the reference program's by a relative error of at most 0.012.
Values may be sent and summed in bfloat16 or wider, within the bound.
A program may use at most 128 MiB of HBM per device.

```python
import jax
import jax.numpy as jnp
from jax import lax

D = 768
HEADS = 12
HEAD_DIM = 64
FF = 3072
SEQ = 197
IMG_DEV = 4
TOKENS = 6304
N_DP = 8


def strengthened(array, stream_key, source, target, parts, factor):
    owner, partner = [(jnp.arange(array.shape[position]) // (array.shape[position] // parts)).reshape([-1 if axis == position else 1 for axis in range(array.ndim)]) for position in (source, target)]
    chosen = jax.random.permutation(stream_key, parts)[partner]
    strong = (owner == chosen) | (owner == (partner + parts // 2) % parts)
    return jnp.where(strong, factor * array, array)


def block_scale(rng, extent, cuts, low, top_value):
    loudness = 1.0
    for axis_at, shards_of in cuts:
        heights = jax.random.uniform(jax.random.fold_in(jax.random.fold_in(rng, 6), axis_at), (shards_of,), jnp.float32, low / len(cuts), top_value / len(cuts))
        loudness = loudness * jnp.repeat(jnp.exp(heights), extent[axis_at] // shards_of).reshape((-1,) + (1,) * (len(extent) - 1 - axis_at))
    return loudness


def bell_draw(rng, shape, scale, reach, shards=(), kind=jnp.bfloat16):
    values = scale * jax.random.normal(rng, shape, jnp.float32)
    if shards:
        values = values * block_scale(rng, shape, shards, -0.22, 0.18)
    return jnp.clip(values, -reach, reach).astype(kind)


def heavy_noise(rng, extent, width, reach, pieces, heavy, dtype=jnp.bfloat16):
    entries = width * jax.random.normal(rng, extent, jnp.float32)
    if pieces:
        entries = entries * block_scale(rng, extent, pieces, -0.22, 0.18)
    return jnp.clip(strengthened(entries, jax.random.fold_in(rng, 3), *heavy), -reach, reach).astype(dtype)


def setup_inputs(seed: int = 0) -> dict:
    key_list = jax.random.split(jax.random.key(seed), 18)
    tokens = bell_draw(key_list[0], (TOKENS, D), 1.0, 6.0, ((0, 32),))
    cotangent = heavy_noise(key_list[1], (TOKENS, D), 1.0, 6.0, ((0, 32),), (0, 1, 32, 2.75))
    ln1_gain = jnp.clip(1.0 + 0.1 * jax.random.normal(key_list[2], (D,), jnp.float32), 0.5, 1.5)
    ln1_bias = bell_draw(key_list[3], (D,), 0.5, 3.0, (), jnp.float32)
    w_query = bell_draw(key_list[4], (D, D), D ** -0.5, 0.21875, ((0, 8), (1, 4)))
    query_bias = bell_draw(key_list[5], (D,), 0.3, 2.0, ((0, 4),), jnp.float32)
    w_key = bell_draw(key_list[6], (D, D), D ** -0.5, 0.21875, ((0, 8), (1, 4)))
    w_value = bell_draw(key_list[7], (D, D), D ** -0.5, 0.21875, ((0, 8), (1, 4)))
    value_bias = bell_draw(key_list[8], (D,), 0.3, 2.0, ((0, 4),), jnp.float32)
    w_out = bell_draw(key_list[9], (D, D), (max(1, 3 * D // SEQ)) ** -0.5, 1.75, ((0, 8), (1, 4)))
    out_bias = bell_draw(key_list[10], (D,), 0.3, 2.0, (), jnp.float32)
    ln2_gain = jnp.clip(1.0 + 0.1 * jax.random.normal(key_list[11], (D,), jnp.float32), 0.5, 1.5)
    ln2_bias = bell_draw(key_list[12], (D,), 0.5, 3.0, (), jnp.float32)
    w_up = bell_draw(key_list[13], (D, FF), D ** -0.5, 0.21875, ((0, 8), (1, 4)))
    up_bias = bell_draw(key_list[14], (FF,), 0.3, 2.0, ((0, 4),), jnp.float32)
    w_down = bell_draw(key_list[15], (D, FF), FF ** -0.5, 0.109375, ((0, 8), (1, 4)))
    down_bias = bell_draw(key_list[16], (D,), 0.3, 2.0, (), jnp.float32)
    return dict(tokens=tokens, cotangent=cotangent, ln1_gain=ln1_gain, ln1_bias=ln1_bias, w_query=w_query, query_bias=query_bias, w_key=w_key, w_value=w_value, value_bias=value_bias, w_out=w_out, out_bias=out_bias, ln2_gain=ln2_gain, ln2_bias=ln2_bias, w_up=w_up, up_bias=up_bias, w_down=w_down, down_bias=down_bias)


highest = lax.Precision.HIGHEST
norm_eps = 1e-06

@jax.custom_vjp
def low(v):
    return lax.optimization_barrier(v.astype(jnp.bfloat16)).astype(jnp.float32)

@jax.custom_vjp
def low_back(v):
    return v

def low_keep(v):
    return (low(v), None)

def low_pass(kept, grad):
    return (grad,)

def back_keep(v):
    return (v, None)

def back_low(kept, grad):
    return (low(grad),)
low.defvjp(low_keep, low_pass)
low_back.defvjp(back_keep, back_low)

def layer_norm(inputs, gain, shift):
    row_mean = lax.optimization_barrier(jnp.mean(inputs, axis=-1, keepdims=True))
    centred = inputs - row_mean
    variance = lax.optimization_barrier(jnp.mean(centred * centred, axis=-1, keepdims=True))
    return centred * lax.rsqrt(variance + norm_eps) * gain + shift

def gelu_exact(upper):
    return jax.nn.gelu(upper, approximate=False)

def attend(block):
    queries, keys, values = block
    scores = low_back(jnp.einsum('bqhd,bkhd->bhqk', queries, keys, precision=highest))
    probs = low(jax.nn.softmax(scores * HEAD_DIM ** (-0.5), axis=-1))
    return jnp.einsum('bhqk,bkhd->bqhd', probs, values, precision=highest)

def forward(tokens, ln1_gain, ln1_bias, w_query, query_bias, w_key, w_value, value_bias, w_out, out_bias, ln2_gain, ln2_bias, w_up, up_bias, w_down, down_bias):
    normed = low(layer_norm(tokens, ln1_gain, ln1_bias))
    queries = low(low_back(jnp.dot(normed, w_query, precision=highest) + query_bias))
    keys = low(low_back(jnp.dot(normed, w_key, precision=highest)))
    values = low(low_back(jnp.dot(normed, w_value, precision=highest) + value_bias))
    block_shape = (N_DP, IMG_DEV, SEQ, HEADS, HEAD_DIM)
    mixed = lax.map(jax.checkpoint(attend), (queries.reshape(block_shape), keys.reshape(block_shape), values.reshape(block_shape)))
    mixed = low(low_back(mixed.reshape(TOKENS, D)))
    branch = low_back(jnp.dot(mixed, w_out.T, precision=highest) + out_bias)
    middle = tokens + branch
    normed2 = low(layer_norm(middle, ln2_gain, ln2_bias))
    upper = low_back(jnp.dot(normed2, w_up, precision=highest) + up_bias)
    hidden = low(gelu_exact(upper))
    branch2 = low_back(jnp.dot(hidden, w_down.T, precision=highest) + down_bias)
    return middle + branch2

def reference(tokens, cotangent, ln1_gain, ln1_bias, w_query, query_bias, w_key, w_value, value_bias, w_out, out_bias, ln2_gain, ln2_bias, w_up, up_bias, w_down, down_bias):
    params = (tokens, ln1_gain, ln1_bias, w_query, query_bias, w_key, w_value, value_bias, w_out, out_bias, ln2_gain, ln2_bias, w_up, up_bias, w_down, down_bias)
    params = tuple((item.astype(jnp.float32) for item in params))
    output, pullback = jax.vjp(forward, *params)
    grads = pullback(cotangent.astype(jnp.float32))
    return (output.astype(jnp.bfloat16), grads[0], grads[1], grads[2], grads[3], grads[4], grads[5], grads[6], grads[7], grads[8], grads[9], grads[10], grads[11], grads[12], grads[13], grads[14], grads[15])
```

```python
import functools

import jax
import jax.numpy as jnp
from jax import lax
from jax.experimental import pallas as pl
from jax.experimental.pallas import tpu as pltpu
from jax.sharding import PartitionSpec as P

HEAD_DIM = 64
SEQ = 197
MESH = pl.DeviceIdType.MESH

norm_eps = 1e-06


def layer_norm(inputs, gain, shift):
    row_mean = jnp.mean(inputs, axis=-1, keepdims=True)
    centred = inputs - row_mean
    variance = jnp.mean(centred * centred, axis=-1, keepdims=True)
    return centred * lax.rsqrt(variance + norm_eps) * gain + shift


def gelu_exact(upper):
    return jax.nn.gelu(upper, approximate=False)


def matmul(left, right):
    return jnp.dot(left, right, preferred_element_type=jnp.float32)


def contract_rows(left, right):
    return lax.dot_general(
        left, right, (((0,), (0,)), ((), ())), preferred_element_type=jnp.float32
    )


def times_transposed(left, right):
    return lax.dot_general(
        left, right, (((1,), (1,)), ((), ())), preferred_element_type=jnp.float32
    )


def column_sums(grads_low):
    return jnp.sum(grads_low.astype(jnp.float32), axis=0)


def flip(index, bit):
    return index + (1 << bit) * (1 - 2 * bit_of(index, bit))


def bit_of(index, bit):
    return lax.rem(lax.div(index, 1 << bit), 2)


def bits_in(size):
    return size.bit_length() - 1


def dp_order(n_bits, variant):
    rest = list(range(1, n_bits))
    if variant:
        rest = rest[::-1]
    return [0] + rest if n_bits else []


def greet(dp, mp, dp_bits, mp_bits):
    barrier = pltpu.get_barrier_semaphore()
    for bit in range(dp_bits):
        pl.semaphore_signal(barrier, inc=1, device_id=(flip(dp, bit), mp), device_id_type=MESH)
    for bit in range(mp_bits):
        pl.semaphore_signal(barrier, inc=1, device_id=(dp, flip(mp, bit)), device_id_type=MESH)
    pl.semaphore_wait(barrier, dp_bits + mp_bits)


def gather_plan(dp_bits, mp_bits, variant):
    stages = []
    done_mp = []
    for bit in range(mp_bits)[::-1]:
        stages.append(("mp", bit, (), tuple(done_mp)))
        done_mp.append(bit)
    done_dp = []
    for bit in dp_order(dp_bits, variant)[::-1]:
        stages.append(("dp", bit, tuple(done_dp), tuple(done_mp)))
        done_dp.append(bit)
    return stages


def subsets(index, handled):
    out = [index]
    for bit in handled:
        out = out + [flip(item, bit) for item in out]
    return out


def gather_kernel(n_dp, n_mp, halves, n_mats, *refs):
    shards, outs = refs[:n_mats], refs[n_mats : 2 * n_mats]
    send_sem, recv_sem, own_sem = refs[2 * n_mats :]
    dp_bits, mp_bits = bits_in(n_dp), bits_in(n_mp)
    rows, width = shards[0].shape
    piece = rows // halves
    dp, mp = lax.axis_index("dp"), lax.axis_index("mp")

    def columns(m):
        return pl.ds(pl.multiple_of(m * width, width), width)

    def part(mat, half, d, m):
        row = pl.ds(half * piece, piece)
        if m is None:
            return outs[mat].at[d, row, :]
        return outs[mat].at[d, row, columns(m)]

    locals_ = []
    for mat in range(n_mats):
        copy = pltpu.make_async_copy(
            shards[mat], outs[mat].at[dp, :, columns(mp)], own_sem.at[mat]
        )
        copy.start()
        locals_.append(copy)
    greet(dp, mp, dp_bits, mp_bits)
    for copy in locals_:
        copy.wait()

    sent = []
    waiting = {}
    n_stages = dp_bits + mp_bits

    def run(mat, half, stage):
        variant = half if halves > 1 else mat % 2
        chunk = mat * halves + half
        axis, bit, done_dp, done_mp = gather_plan(dp_bits, mp_bits, variant)[stage]
        if axis == "mp":
            mine = [(dp, m) for m in subsets(mp, done_mp)]
            theirs = [(dp, m) for m in subsets(flip(mp, bit), done_mp)]
            target = (dp, flip(mp, bit))
        else:
            mine = [(d, None) for d in subsets(dp, done_dp)]
            theirs = [(d, None) for d in subsets(flip(dp, bit), done_dp)]
            target = (flip(dp, bit), mp)
        slot = 0
        for earlier in range(stage):
            _, _, e_dp, e_mp = gather_plan(dp_bits, mp_bits, variant)[earlier]
            slot += 1 << (len(e_mp) if earlier < mp_bits else len(e_dp))
        for number, ((d, m), (their_d, their_m)) in enumerate(zip(mine, theirs)):
            sems = dict(
                send_sem=send_sem.at[chunk, slot + number],
                recv_sem=recv_sem.at[chunk, slot + number],
                device_id=target,
                device_id_type=MESH,
            )
            source = part(mat, half, d, m)
            copy = pltpu.make_async_remote_copy(src_ref=source, dst_ref=source, **sems)
            copy.start()
            sent.append(copy)
            landing = part(mat, half, their_d, their_m)
            waiting.setdefault((mat, half), []).append(
                pltpu.make_async_remote_copy(src_ref=landing, dst_ref=landing, **sems)
            )

    def settle(mat, half):
        for copy in waiting.pop((mat, half), []):
            copy.wait_recv()

    for step in range(n_mats + n_stages):
        for stage in range(n_stages + 1)[::-1]:
            mat = step - stage
            if 0 <= mat < n_mats:
                for half in range(halves):
                    settle(mat, half)
                    if stage < n_stages:
                        run(mat, half, stage)
    for copy in sent:
        copy.wait_send()


def gather_weights(shards, n_dp, n_mp):
    rows, width = shards[0].shape
    n_mats = len(shards)
    halves = 2 if rows % 32 == 0 else 1
    copies = (n_mp - 1) + (n_dp - 1)
    return pl.pallas_call(
        functools.partial(gather_kernel, n_dp, n_mp, halves, n_mats),
        out_shape=[jax.ShapeDtypeStruct((n_dp, rows, n_mp * width), jnp.bfloat16)] * n_mats,
        in_specs=[pl.BlockSpec(memory_space=pl.ANY)] * n_mats,
        out_specs=[pl.BlockSpec(memory_space=pl.ANY)] * n_mats,
        scratch_shapes=[
            pltpu.SemaphoreType.DMA((n_mats * halves, copies)),
            pltpu.SemaphoreType.DMA((n_mats * halves, copies)),
            pltpu.SemaphoreType.DMA((n_mats,)),
        ],
        compiler_params=pltpu.CompilerParams(collective_id=0, has_side_effects=True),
    )(*shards)


def reduce_kernel(n_dp, n_mp, halves, n_mats, *refs):
    parts, vectors = refs[:n_mats], refs[n_mats]
    sums, vector_sum = refs[n_mats + 1 : n_mats + 3]
    dp_bits, mp_bits = bits_in(n_dp), bits_in(n_mp)
    n_stages = dp_bits + mp_bits
    scratch = refs[n_mats + 3 :]
    kept = scratch[0]
    landed = scratch[1 : 1 + n_stages]
    vector_in = scratch[1 + n_stages]
    vector_at = scratch[2 + n_stages]
    send_sem, recv_sem, kept_sem, v_send, v_recv = scratch[3 + n_stages :]
    rows = sums.shape[1]
    width = sums.shape[2]
    piece = rows // halves
    group = 16 if piece % 16 == 0 else piece
    dp, mp = lax.axis_index("dp"), lax.axis_index("mp")

    def arranged(order, fixed_bit, value):
        out = [value * (1 << fixed_bit)]
        for bit in order:
            out = [item + (side << bit) for item in out for side in (0, 1)]
        return out

    greet(dp, mp, dp_bits, mp_bits)
    vector_at[0] = vectors[...]
    sent = []
    waiting = {}
    vector_wait = []

    def partner(axis, bit):
        if axis == "dp":
            return (flip(dp, bit), mp)
        return (dp, flip(mp, bit))

    def stages_of(variant):
        order = dp_order(dp_bits, variant)
        return [("dp", bit) for bit in order] + [("mp", bit) for bit in range(mp_bits)]

    def send(key, source, landing, sem, target):
        copy = pltpu.make_async_remote_copy(
            src_ref=source,
            dst_ref=landing,
            send_sem=send_sem.at[sem],
            recv_sem=recv_sem.at[sem],
            device_id=target,
            device_id_type=MESH,
        )
        copy.start()
        sent.append(copy)
        waiting.setdefault(key, []).append(copy)

    first = n_dp // 2

    def run(mat, half, stage):
        variant = half if halves > 1 else mat % 2
        chunk = mat * halves + half
        plan = stages_of(variant)
        axis, bit = plan[stage]
        target = partner(axis, bit)
        key = (mat, half)
        row = pl.ds(half * piece, piece)
        if stage == 0:
            order = [b for _, b in plan[1:dp_bits]]
            side = bit_of(dp, bit)
            for number, block in enumerate(arranged(order, bit, 1 - side)):
                send(
                    key,
                    parts[mat].at[block, row, :],
                    landed[0].at[chunk, number],
                    (chunk, number),
                    target,
                )
            for number, block in enumerate(arranged(order, bit, side)):
                copy = pltpu.make_async_copy(
                    parts[mat].at[block, row, :], kept.at[chunk, number], kept_sem.at[chunk, number]
                )
                copy.start()
                waiting[key].append(copy)
        elif axis == "dp":
            count = n_dp >> (stage + 1)
            start = (1 - bit_of(dp, bit)) * count
            send(
                key,
                landed[stage - 1].at[chunk, pl.ds(start, count)],
                landed[stage].at[chunk],
                (chunk, first + stage - 1),
                target,
            )
        else:
            count = n_mp >> (bit + 1)
            slot = first + dp_bits - 1 + (n_mp - (n_mp >> bit))
            for number in range(count):
                block = 2 * number + 1 - bit_of(mp, bit)
                send(
                    key,
                    landed[stage - 1].at[chunk, 0, :, pl.ds(pl.multiple_of(block * width, width), width)],
                    landed[stage].at[chunk, 0, :, pl.ds(number * width, width)],
                    (chunk, slot + number),
                    target,
                )

    def settle(mat, half, stage):
        variant = half if halves > 1 else mat % 2
        chunk = mat * halves + half
        for copy in waiting.pop((mat, half)):
            if hasattr(copy, "wait_recv") and copy.is_remote:
                copy.wait_recv()
            else:
                copy.wait()
        axis, bit = stages_of(variant)[stage]
        last = stage == n_stages - 1
        into = landed[stage]
        blocks = into.shape[1]

        @pl.loop(0, blocks * (piece // group))
        def _(at):
            block = lax.div(at, piece // group)
            start = lax.rem(at, piece // group) * group
            if group % 16 == 0:
                start = pl.multiple_of(start, group)
            here = pl.ds(start, group)
            if axis == "dp":
                if stage == 0:
                    own = kept[chunk, block, here, :]
                else:
                    base = bit_of(dp, bit) * blocks
                    own = landed[stage - 1][chunk, base + block, here, :]
                total = own.astype(jnp.float32) + into[chunk, block, here, :].astype(jnp.float32)
                into[chunk, block, here, :] = total.astype(jnp.bfloat16)
            else:
                for number in range(n_mp >> (bit + 1)):
                    source = 2 * number + bit_of(mp, bit)
                    own = landed[stage - 1][
                        chunk, 0, here, pl.ds(pl.multiple_of(source * width, width), width)
                    ]
                    cols = pl.ds(number * width, width)
                    total = own.astype(jnp.float32) + into[chunk, 0, here, cols].astype(jnp.float32)
                    if last:
                        place = pl.ds(half * piece + start, group)
                        sums[mat, place, :] = total
                    else:
                        into[chunk, 0, here, cols] = total.astype(jnp.bfloat16)

    vector_plan = stages_of(0)

    def vector_send(stage):
        axis, bit = vector_plan[stage]
        copy = pltpu.make_async_remote_copy(
            src_ref=vector_at.at[stage],
            dst_ref=vector_in.at[stage],
            send_sem=v_send.at[stage],
            recv_sem=v_recv.at[stage],
            device_id=partner(axis, bit),
            device_id_type=MESH,
        )
        copy.start()
        vector_wait.append(copy)

    def vector_settle(stage):
        vector_wait[stage].wait()
        total = vector_at[stage] + vector_in[stage]
        if stage == n_stages - 1:
            vector_sum[...] = total
        else:
            vector_at[stage + 1] = total

    for step in range(n_mats + n_stages):
        if 1 <= step <= n_stages:
            vector_settle(step - 1)
        if step < n_stages:
            vector_send(step)
        for stage in range(n_stages + 1)[::-1]:
            mat = step - stage
            if 0 <= mat < n_mats:
                for half in range(halves):
                    if stage > 0:
                        settle(mat, half, stage - 1)
                    if stage < n_stages:
                        run(mat, half, stage)
    for copy in sent:
        copy.wait_send()


def reduce_gradients(parts, vectors, n_dp, n_mp):
    n_mats = len(parts)
    _, rows, full = parts[0].shape
    width = full // n_mp
    halves = 2 if rows % 32 == 0 else 1
    piece = rows // halves
    chunks = n_mats * halves
    dp_bits, mp_bits = bits_in(n_dp), bits_in(n_mp)
    n_stages = dp_bits + mp_bits
    landings = [
        pltpu.VMEM((chunks, n_dp >> (stage + 1), piece, full), jnp.bfloat16)
        for stage in range(dp_bits)
    ] + [
        pltpu.VMEM((chunks, 1, piece, full >> (stage + 1)), jnp.bfloat16)
        for stage in range(mp_bits)
    ]
    copies = n_dp // 2 + dp_bits - 1 + n_mp - 1
    return pl.pallas_call(
        functools.partial(reduce_kernel, n_dp, n_mp, halves, n_mats),
        out_shape=[
            jax.ShapeDtypeStruct((n_mats, rows, width), jnp.float32),
            jax.ShapeDtypeStruct(vectors.shape, jnp.float32),
        ],
        in_specs=[pl.BlockSpec(memory_space=pl.ANY)] * n_mats
        + [pl.BlockSpec(memory_space=pltpu.VMEM)],
        out_specs=[pl.BlockSpec(memory_space=pltpu.VMEM)] * 2,
        scratch_shapes=[
            pltpu.VMEM((chunks, n_dp // 2, piece, full), jnp.bfloat16),
            *landings,
            pltpu.VMEM((n_stages,) + vectors.shape, jnp.float32),
            pltpu.VMEM((n_stages,) + vectors.shape, jnp.float32),
            pltpu.SemaphoreType.DMA((chunks, copies)),
            pltpu.SemaphoreType.DMA((chunks, copies)),
            pltpu.SemaphoreType.DMA((chunks, n_dp // 2)),
            pltpu.SemaphoreType.DMA((n_stages,)),
            pltpu.SemaphoreType.DMA((n_stages,)),
        ],
        compiler_params=pltpu.CompilerParams(
            collective_id=1, has_side_effects=True, vmem_limit_bytes=48 * 1024 * 1024
        ),
    )(*parts, vectors)


def per_device(
    n_dp,
    n_mp,
    tokens,
    cotangent,
    ln1_gain,
    ln1_bias,
    w_query,
    query_bias,
    w_key,
    w_value,
    value_bias,
    w_out,
    out_bias,
    ln2_gain,
    ln2_bias,
    w_up,
    up_bias,
    w_down,
    down_bias,
):
    own_rows, width = tokens.shape
    images = own_rows // SEQ
    rows, local = w_query.shape
    heads = width // HEAD_DIM
    scale = HEAD_DIM ** (-0.5)
    head_shape = (images, SEQ, heads, HEAD_DIM)
    attn_shard = jnp.concatenate([w_query, w_key, w_value, w_out], axis=1)
    attn, up, down = (
        full.reshape(n_dp * rows, -1)
        for full in gather_weights((attn_shard, w_up, w_down), n_dp, n_mp)
    )
    both = lax.all_gather(jnp.concatenate([query_bias, value_bias, up_bias]), "mp", axis=0)
    query_bias = both[:, :local].reshape(-1)
    value_bias = both[:, local : 2 * local].reshape(-1)
    up_bias = both[:, 2 * local :].reshape(-1)

    def interleave(*slots):
        return jnp.stack([s.reshape(own_rows, n_mp, local) for s in slots], axis=2).reshape(
            own_rows, -1
        )

    def slot_of(array, slot):
        return array.reshape(own_rows, n_mp, 4, local)[:, :, slot].reshape(own_rows, width)

    inputs = tokens.astype(jnp.float32)
    normed_f, norm1_back = jax.vjp(layer_norm, inputs, ln1_gain, ln1_bias)
    normed = normed_f.astype(jnp.bfloat16)
    projected = matmul(normed, attn)
    queries = (slot_of(projected, 0) + query_bias).astype(jnp.bfloat16).reshape(head_shape)
    keys_low = slot_of(projected, 1).astype(jnp.bfloat16).reshape(head_shape)
    values_low = (slot_of(projected, 2) + value_bias).astype(jnp.bfloat16).reshape(head_shape)
    scaled = (
        jnp.einsum("bqhd,bkhd->bhqk", queries, keys_low, preferred_element_type=jnp.float32) * scale
    )
    row_top = jnp.max(scaled, axis=-1, keepdims=True)
    expos = jnp.exp(scaled - row_top)
    probs = expos / jnp.sum(expos, axis=-1, keepdims=True)
    probs_low = probs.astype(jnp.bfloat16)
    mixed = jnp.einsum("bhqk,bkhd->bqhd", probs_low, values_low, preferred_element_type=jnp.float32)
    mixed = mixed.reshape(own_rows, width).astype(jnp.bfloat16)
    none = jnp.zeros_like(mixed)
    mixed_slots = interleave(none, none, none, mixed)
    middle = inputs + (times_transposed(mixed_slots, attn) + out_bias)
    normed2_f, norm2_back = jax.vjp(layer_norm, middle, ln2_gain, ln2_bias)
    normed2 = normed2_f.astype(jnp.bfloat16)
    upper = matmul(normed2, up) + up_bias
    hidden_f, gelu_back = jax.vjp(gelu_exact, upper)
    hidden = hidden_f.astype(jnp.bfloat16)
    output = middle + (times_transposed(hidden, down) + down_bias)
    activations = output.astype(jnp.bfloat16)
    grad_out = cotangent.astype(jnp.float32)
    grad_branch2 = cotangent
    down_bias_part = column_sums(grad_branch2)
    down_part = contract_rows(grad_branch2, hidden).astype(jnp.bfloat16)
    grad_upper = gelu_back(matmul(grad_branch2, down))[0].astype(jnp.bfloat16)
    up_bias_part = column_sums(grad_upper)
    up_part = contract_rows(normed2, grad_upper).astype(jnp.bfloat16)
    grad_normed2 = times_transposed(grad_upper, up)
    grad_mid_norm, ln2_gain_part, ln2_bias_part = norm2_back(grad_normed2)
    grad_middle = grad_out + grad_mid_norm
    grad_branch = grad_middle.astype(jnp.bfloat16)
    out_bias_part = column_sums(grad_branch)
    grad_mixed = slot_of(matmul(grad_branch, attn), 3).astype(jnp.bfloat16).reshape(head_shape)
    grad_probs = jnp.einsum(
        "bqhd,bkhd->bhqk", grad_mixed, values_low, preferred_element_type=jnp.float32
    )
    grad_values = jnp.einsum(
        "bhqk,bqhd->bkhd", probs_low, grad_mixed, preferred_element_type=jnp.float32
    )
    grad_values = grad_values.astype(jnp.bfloat16).reshape(own_rows, width)
    inner = jnp.sum(probs * grad_probs, axis=-1, keepdims=True)
    grad_scores = (probs * (grad_probs - inner) * scale).astype(jnp.bfloat16)
    grad_queries = jnp.einsum(
        "bhqk,bkhd->bqhd", grad_scores, keys_low, preferred_element_type=jnp.float32
    )
    grad_queries = grad_queries.astype(jnp.bfloat16).reshape(own_rows, width)
    grad_keys = jnp.einsum(
        "bhqk,bqhd->bkhd", grad_scores, queries, preferred_element_type=jnp.float32
    )
    grad_keys = grad_keys.astype(jnp.bfloat16).reshape(own_rows, width)
    query_bias_part = column_sums(grad_queries)
    value_bias_part = column_sums(grad_values)
    grad_slots = interleave(grad_queries, grad_keys, grad_values, none)
    attn_part = contract_rows(
        jnp.concatenate([normed, grad_branch], axis=0),
        jnp.concatenate([grad_slots, mixed_slots], axis=0),
    ).astype(jnp.bfloat16)
    grad_normed = times_transposed(grad_slots, attn)
    grad_in_norm, ln1_gain_part, ln1_bias_part = norm1_back(grad_normed)
    input_grad = grad_middle + grad_in_norm
    vectors = jnp.concatenate(
        [
            ln1_gain_part,
            ln1_bias_part,
            out_bias_part,
            ln2_gain_part,
            ln2_bias_part,
            down_bias_part,
            query_bias_part,
            value_bias_part,
            up_bias_part,
        ]
    ).reshape(-1, width)
    sums, vector_sums = reduce_gradients(
        [part.reshape(n_dp, rows, -1) for part in (down_part, up_part, attn_part)],
        vectors,
        n_dp,
        n_mp,
    )
    at = lax.axis_index("mp")
    up_width = w_up.shape[1]
    own_up = lax.dynamic_slice_in_dim(vector_sums[8:].reshape(-1), at * up_width, up_width)
    return (
        activations,
        input_grad,
        vector_sums[0],
        vector_sums[1],
        sums[2, :, :local],
        lax.dynamic_slice_in_dim(vector_sums[6], at * local, local),
        sums[2, :, local : 2 * local],
        sums[2, :, 2 * local : 3 * local],
        lax.dynamic_slice_in_dim(vector_sums[7], at * local, local),
        sums[2, :, 3 * local :],
        vector_sums[2],
        vector_sums[3],
        vector_sums[4],
        sums[1],
        own_up,
        sums[0],
        vector_sums[5],
    )


def solution(mesh):
    whole, rows, block, ends = P(), P(("dp", "mp"), None), P("dp", "mp"), P("mp")
    in_specs = (
        rows, rows, whole, whole, block, ends, block, block, ends, block,
        whole, whole, whole, block, ends, block, whole,
    )
    out_specs = (
        rows, rows, whole, whole, block, ends, block, block, ends, block,
        whole, whole, whole, block, ends, block, whole,
    )
    return jax.shard_map(
        functools.partial(per_device, mesh.shape["dp"], mesh.shape["mp"]),
        mesh=mesh,
        in_specs=in_specs,
        out_specs=out_specs,
        check_vma=False,
    )
```

```python
import functools

import jax
import jax.numpy as jnp
from jax import lax
from jax.experimental import pallas as pl
from jax.experimental.pallas import tpu as pltpu
from jax.sharding import PartitionSpec as P

HEAD_DIM = 64
SEQ = 197
MESH = pl.DeviceIdType.MESH

norm_eps = 1e-06


def layer_norm(inputs, gain, shift):
    row_mean = jnp.mean(inputs, axis=-1, keepdims=True)
    centred = inputs - row_mean
    variance = jnp.mean(centred * centred, axis=-1, keepdims=True)
    return centred * lax.rsqrt(variance + norm_eps) * gain + shift


def gelu_exact(upper):
    return jax.nn.gelu(upper, approximate=False)


def matmul(left, right):
    return jnp.dot(left, right, preferred_element_type=jnp.float32)


def contract_rows(left, right):
    return lax.dot_general(
        left, right, (((0,), (0,)), ((), ())), preferred_element_type=jnp.float32
    )


def times_transposed(left, right):
    return lax.dot_general(
        left, right, (((1,), (1,)), ((), ())), preferred_element_type=jnp.float32
    )


def column_sums(grads_low):
    return jnp.sum(grads_low.astype(jnp.float32), axis=0)


def flip(index, bit):
    return index + (1 << bit) * (1 - 2 * bit_of(index, bit))


def bit_of(index, bit):
    return lax.rem(lax.div(index, 1 << bit), 2)


def bits_in(size):
    return size.bit_length() - 1


def dp_order(n_bits, variant):
    rest = list(range(1, n_bits))
    if variant:
        rest = rest[::-1]
    return [0] + rest if n_bits else []


def greet(dp, mp, dp_bits, mp_bits):
    barrier = pltpu.get_barrier_semaphore()
    for bit in range(dp_bits):
        pl.semaphore_signal(barrier, inc=1, device_id=(flip(dp, bit), mp), device_id_type=MESH)
    for bit in range(mp_bits):
        pl.semaphore_signal(barrier, inc=1, device_id=(dp, flip(mp, bit)), device_id_type=MESH)
    pl.semaphore_wait(barrier, dp_bits + mp_bits)


def gather_plan(dp_bits, mp_bits, variant):
    stages = []
    done_mp = []
    for bit in range(mp_bits)[::-1]:
        stages.append(("mp", bit, (), tuple(done_mp)))
        done_mp.append(bit)
    done_dp = []
    for bit in dp_order(dp_bits, variant)[::-1]:
        stages.append(("dp", bit, tuple(done_dp), tuple(done_mp)))
        done_dp.append(bit)
    return stages


def subsets(index, handled):
    out = [index]
    for bit in handled:
        out = out + [flip(item, bit) for item in out]
    return out


def gather_kernel(n_dp, n_mp, halves, n_mats, *refs):
    shards, bias = refs[:n_mats], refs[n_mats]
    outs, bias_all = refs[n_mats + 1 : 2 * n_mats + 1], refs[2 * n_mats + 1]
    send_sem, recv_sem, own_sem, bias_send, bias_recv = refs[2 * n_mats + 2 :]
    dp_bits, mp_bits = bits_in(n_dp), bits_in(n_mp)
    rows, width = shards[0].shape
    piece = rows // halves
    dp, mp = lax.axis_index("dp"), lax.axis_index("mp")

    def columns(m):
        return pl.ds(pl.multiple_of(m * width, width), width)

    def part(mat, half, d, m):
        row = pl.ds(half * piece, piece)
        if m is None:
            return outs[mat].at[d, row, :]
        return outs[mat].at[d, row, columns(m)]

    locals_ = []
    for mat in range(n_mats):
        copy = pltpu.make_async_copy(
            shards[mat], outs[mat].at[dp, :, columns(mp)], own_sem.at[mat]
        )
        copy.start()
        locals_.append(copy)
    greet(dp, mp, dp_bits, mp_bits)
    for copy in locals_:
        copy.wait()

    sent = []
    waiting = {}
    n_stages = dp_bits + mp_bits
    bias_all[mp] = bias[...]
    bias_wait = []

    def bias_run(stage):
        _, bit, _, done_mp = gather_plan(dp_bits, mp_bits, 0)[stage]
        slot = (1 << stage) - 1
        for number, (m, their_m) in enumerate(
            zip(subsets(mp, done_mp), subsets(flip(mp, bit), done_mp))
        ):
            sems = dict(
                send_sem=bias_send.at[slot + number],
                recv_sem=bias_recv.at[slot + number],
                device_id=(dp, flip(mp, bit)),
                device_id_type=MESH,
            )
            copy = pltpu.make_async_remote_copy(
                src_ref=bias_all.at[m], dst_ref=bias_all.at[m], **sems
            )
            copy.start()
            sent.append(copy)
            bias_wait.append(
                pltpu.make_async_remote_copy(
                    src_ref=bias_all.at[their_m], dst_ref=bias_all.at[their_m], **sems
                )
            )

    def run(mat, half, stage):
        variant = half if halves > 1 else mat % 2
        chunk = mat * halves + half
        axis, bit, done_dp, done_mp = gather_plan(dp_bits, mp_bits, variant)[stage]
        if axis == "mp":
            mine = [(dp, m) for m in subsets(mp, done_mp)]
            theirs = [(dp, m) for m in subsets(flip(mp, bit), done_mp)]
            target = (dp, flip(mp, bit))
        else:
            mine = [(d, None) for d in subsets(dp, done_dp)]
            theirs = [(d, None) for d in subsets(flip(dp, bit), done_dp)]
            target = (flip(dp, bit), mp)
        slot = 0
        for earlier in range(stage):
            _, _, e_dp, e_mp = gather_plan(dp_bits, mp_bits, variant)[earlier]
            slot += 1 << (len(e_mp) if earlier < mp_bits else len(e_dp))
        for number, ((d, m), (their_d, their_m)) in enumerate(zip(mine, theirs)):
            sems = dict(
                send_sem=send_sem.at[chunk, slot + number],
                recv_sem=recv_sem.at[chunk, slot + number],
                device_id=target,
                device_id_type=MESH,
            )
            source = part(mat, half, d, m)
            copy = pltpu.make_async_remote_copy(src_ref=source, dst_ref=source, **sems)
            copy.start()
            sent.append(copy)
            landing = part(mat, half, their_d, their_m)
            waiting.setdefault((mat, half), []).append(
                pltpu.make_async_remote_copy(src_ref=landing, dst_ref=landing, **sems)
            )

    def settle(mat, half):
        for copy in waiting.pop((mat, half), []):
            copy.wait_recv()

    for step in range(n_mats + n_stages):
        if step <= mp_bits:
            while bias_wait:
                bias_wait.pop().wait_recv()
            if step < mp_bits:
                bias_run(step)
        for stage in range(n_stages + 1)[::-1]:
            mat = step - stage
            if 0 <= mat < n_mats:
                for half in range(halves):
                    settle(mat, half)
                    if stage < n_stages:
                        run(mat, half, stage)
    for copy in sent:
        copy.wait_send()


def gather_weights(shards, bias, n_dp, n_mp):
    rows, width = shards[0].shape
    n_mats = len(shards)
    halves = 2 if rows % 32 == 0 else 1
    copies = (n_mp - 1) + (n_dp - 1)
    return pl.pallas_call(
        functools.partial(gather_kernel, n_dp, n_mp, halves, n_mats),
        out_shape=[jax.ShapeDtypeStruct((n_dp, rows, n_mp * width), jnp.bfloat16)] * n_mats
        + [jax.ShapeDtypeStruct((n_mp,) + bias.shape, jnp.float32)],
        in_specs=[pl.BlockSpec(memory_space=pl.ANY)] * n_mats
        + [pl.BlockSpec(memory_space=pltpu.VMEM)],
        out_specs=[pl.BlockSpec(memory_space=pl.ANY)] * n_mats
        + [pl.BlockSpec(memory_space=pltpu.VMEM)],
        scratch_shapes=[
            pltpu.SemaphoreType.DMA((n_mats * halves, copies)),
            pltpu.SemaphoreType.DMA((n_mats * halves, copies)),
            pltpu.SemaphoreType.DMA((n_mats,)),
            pltpu.SemaphoreType.DMA((max(n_mp - 1, 1),)),
            pltpu.SemaphoreType.DMA((max(n_mp - 1, 1),)),
        ],
        compiler_params=pltpu.CompilerParams(collective_id=0, has_side_effects=True),
    )(*shards, bias)


def reduce_kernel(n_dp, n_mp, halves, n_mats, *refs):
    parts, vectors = refs[:n_mats], refs[n_mats]
    sums, vector_sum = refs[n_mats + 1 : n_mats + 3]
    dp_bits, mp_bits = bits_in(n_dp), bits_in(n_mp)
    n_stages = dp_bits + mp_bits
    scratch = refs[n_mats + 3 :]
    kept = scratch[0]
    landed = scratch[1 : 1 + n_stages]
    vector_in = scratch[1 + n_stages]
    vector_at = scratch[2 + n_stages]
    send_sem, recv_sem, kept_sem, v_send, v_recv = scratch[3 + n_stages :]
    rows = sums.shape[1]
    width = sums.shape[2]
    piece = rows // halves
    group = 16 if piece % 16 == 0 else piece
    dp, mp = lax.axis_index("dp"), lax.axis_index("mp")

    def arranged(order, fixed_bit, value):
        out = [value * (1 << fixed_bit)]
        for bit in order:
            out = [item + (side << bit) for item in out for side in (0, 1)]
        return out

    greet(dp, mp, dp_bits, mp_bits)
    vector_at[0] = vectors[...]
    sent = []
    waiting = {}
    vector_wait = []

    def partner(axis, bit):
        if axis == "dp":
            return (flip(dp, bit), mp)
        return (dp, flip(mp, bit))

    def stages_of(variant):
        order = dp_order(dp_bits, variant)
        return [("dp", bit) for bit in order] + [("mp", bit) for bit in range(mp_bits)]

    def send(key, source, landing, sem, target):
        copy = pltpu.make_async_remote_copy(
            src_ref=source,
            dst_ref=landing,
            send_sem=send_sem.at[sem],
            recv_sem=recv_sem.at[sem],
            device_id=target,
            device_id_type=MESH,
        )
        copy.start()
        sent.append(copy)
        waiting.setdefault(key, []).append(copy)

    first = n_dp // 2

    def run(mat, half, stage):
        variant = half if halves > 1 else mat % 2
        chunk = mat * halves + half
        plan = stages_of(variant)
        axis, bit = plan[stage]
        target = partner(axis, bit)
        key = (mat, half)
        row = pl.ds(half * piece, piece)
        if stage == 0:
            order = [b for _, b in plan[1:dp_bits]]
            side = bit_of(dp, bit)
            for number, block in enumerate(arranged(order, bit, 1 - side)):
                send(
                    key,
                    parts[mat].at[block, row, :],
                    landed[0].at[chunk, number],
                    (chunk, number),
                    target,
                )
            for number, block in enumerate(arranged(order, bit, side)):
                copy = pltpu.make_async_copy(
                    parts[mat].at[block, row, :], kept.at[chunk, number], kept_sem.at[chunk, number]
                )
                copy.start()
                waiting[key].append(copy)
        elif axis == "dp":
            count = n_dp >> (stage + 1)
            start = (1 - bit_of(dp, bit)) * count
            send(
                key,
                landed[stage - 1].at[chunk, pl.ds(start, count)],
                landed[stage].at[chunk],
                (chunk, first + stage - 1),
                target,
            )
        else:
            count = n_mp >> (bit + 1)
            slot = first + dp_bits - 1 + (n_mp - (n_mp >> bit))
            for number in range(count):
                block = 2 * number + 1 - bit_of(mp, bit)
                send(
                    key,
                    landed[stage - 1].at[chunk, 0, :, pl.ds(pl.multiple_of(block * width, width), width)],
                    landed[stage].at[chunk, 0, :, pl.ds(number * width, width)],
                    (chunk, slot + number),
                    target,
                )

    def settle(mat, half, stage):
        variant = half if halves > 1 else mat % 2
        chunk = mat * halves + half
        for copy in waiting.pop((mat, half)):
            if hasattr(copy, "wait_recv") and copy.is_remote:
                copy.wait_recv()
            else:
                copy.wait()
        axis, bit = stages_of(variant)[stage]
        last = stage == n_stages - 1
        into = landed[stage]
        blocks = into.shape[1]

        @pl.loop(0, blocks * (piece // group))
        def _(at):
            block = lax.div(at, piece // group)
            start = lax.rem(at, piece // group) * group
            if group % 16 == 0:
                start = pl.multiple_of(start, group)
            here = pl.ds(start, group)
            if axis == "dp":
                if stage == 0:
                    own = kept[chunk, block, here, :]
                else:
                    base = bit_of(dp, bit) * blocks
                    own = landed[stage - 1][chunk, base + block, here, :]
                total = own.astype(jnp.float32) + into[chunk, block, here, :].astype(jnp.float32)
                into[chunk, block, here, :] = total.astype(jnp.bfloat16)
            else:
                for number in range(n_mp >> (bit + 1)):
                    source = 2 * number + bit_of(mp, bit)
                    own = landed[stage - 1][
                        chunk, 0, here, pl.ds(pl.multiple_of(source * width, width), width)
                    ]
                    cols = pl.ds(number * width, width)
                    total = own.astype(jnp.float32) + into[chunk, 0, here, cols].astype(jnp.float32)
                    if last:
                        place = pl.ds(half * piece + start, group)
                        sums[mat, place, :] = total
                    else:
                        into[chunk, 0, here, cols] = total.astype(jnp.bfloat16)

    vector_plan = stages_of(0)

    def vector_send(stage):
        axis, bit = vector_plan[stage]
        copy = pltpu.make_async_remote_copy(
            src_ref=vector_at.at[stage],
            dst_ref=vector_in.at[stage],
            send_sem=v_send.at[stage],
            recv_sem=v_recv.at[stage],
            device_id=partner(axis, bit),
            device_id_type=MESH,
        )
        copy.start()
        vector_wait.append(copy)

    def vector_settle(stage):
        vector_wait[stage].wait()
        total = vector_at[stage] + vector_in[stage]
        if stage == n_stages - 1:
            vector_sum[...] = total
        else:
            vector_at[stage + 1] = total

    for step in range(n_mats + n_stages):
        if 1 <= step <= n_stages:
            vector_settle(step - 1)
        if step < n_stages:
            vector_send(step)
        for stage in range(n_stages + 1)[::-1]:
            mat = step - stage
            if 0 <= mat < n_mats:
                for half in range(halves):
                    if stage > 0:
                        settle(mat, half, stage - 1)
                    if stage < n_stages:
                        run(mat, half, stage)
    for copy in sent:
        copy.wait_send()


def reduce_gradients(parts, vectors, n_dp, n_mp):
    n_mats = len(parts)
    _, rows, full = parts[0].shape
    width = full // n_mp
    halves = 2 if rows % 32 == 0 else 1
    piece = rows // halves
    chunks = n_mats * halves
    dp_bits, mp_bits = bits_in(n_dp), bits_in(n_mp)
    n_stages = dp_bits + mp_bits
    landings = [
        pltpu.VMEM((chunks, n_dp >> (stage + 1), piece, full), jnp.bfloat16)
        for stage in range(dp_bits)
    ] + [
        pltpu.VMEM((chunks, 1, piece, full >> (stage + 1)), jnp.bfloat16)
        for stage in range(mp_bits)
    ]
    copies = n_dp // 2 + dp_bits - 1 + n_mp - 1
    return pl.pallas_call(
        functools.partial(reduce_kernel, n_dp, n_mp, halves, n_mats),
        out_shape=[
            jax.ShapeDtypeStruct((n_mats, rows, width), jnp.float32),
            jax.ShapeDtypeStruct(vectors.shape, jnp.float32),
        ],
        in_specs=[pl.BlockSpec(memory_space=pl.ANY)] * n_mats
        + [pl.BlockSpec(memory_space=pltpu.VMEM)],
        out_specs=[pl.BlockSpec(memory_space=pltpu.VMEM)] * 2,
        scratch_shapes=[
            pltpu.VMEM((chunks, n_dp // 2, piece, full), jnp.bfloat16),
            *landings,
            pltpu.VMEM((n_stages,) + vectors.shape, jnp.float32),
            pltpu.VMEM((n_stages,) + vectors.shape, jnp.float32),
            pltpu.SemaphoreType.DMA((chunks, copies)),
            pltpu.SemaphoreType.DMA((chunks, copies)),
            pltpu.SemaphoreType.DMA((chunks, n_dp // 2)),
            pltpu.SemaphoreType.DMA((n_stages,)),
            pltpu.SemaphoreType.DMA((n_stages,)),
        ],
        compiler_params=pltpu.CompilerParams(
            collective_id=1, has_side_effects=True, vmem_limit_bytes=48 * 1024 * 1024
        ),
    )(*parts, vectors)


def per_device(
    n_dp,
    n_mp,
    tokens,
    cotangent,
    ln1_gain,
    ln1_bias,
    w_query,
    query_bias,
    w_key,
    w_value,
    value_bias,
    w_out,
    out_bias,
    ln2_gain,
    ln2_bias,
    w_up,
    up_bias,
    w_down,
    down_bias,
):
    own_rows, width = tokens.shape
    images = own_rows // SEQ
    rows, local = w_query.shape
    heads = width // HEAD_DIM
    scale = HEAD_DIM ** (-0.5)
    head_shape = (images, SEQ, heads, HEAD_DIM)
    attn_shard = jnp.concatenate([w_query, w_key, w_value, w_out], axis=1)
    bias = jnp.concatenate([query_bias, value_bias, up_bias])
    *weights, both = gather_weights((attn_shard, w_up, w_down), bias.reshape(-1, 128), n_dp, n_mp)
    attn, up, down = (full.reshape(n_dp * rows, -1) for full in weights)
    both = both.reshape(n_mp, -1)
    query_bias = both[:, :local].reshape(-1)
    value_bias = both[:, local : 2 * local].reshape(-1)
    up_bias = both[:, 2 * local :].reshape(-1)

    near = local // HEAD_DIM

    def interleave(*slots):
        stacked = jnp.stack(
            [s.reshape(images, n_mp, near, SEQ, HEAD_DIM) for s in slots], axis=2
        )
        return stacked.transpose(0, 4, 1, 2, 3, 5).reshape(own_rows, -1)

    def slot_of(array, slot):
        return array.reshape(own_rows, n_mp, 4, local)[:, :, slot].reshape(own_rows, width)

    inputs = tokens.astype(jnp.float32)
    normed_f, norm1_back = jax.vjp(layer_norm, inputs, ln1_gain, ln1_bias)
    normed = normed_f.astype(jnp.bfloat16)
    projected = matmul(normed, attn)
    queries = (slot_of(projected, 0) + query_bias).astype(jnp.bfloat16).reshape(head_shape)
    keys_low = slot_of(projected, 1).astype(jnp.bfloat16).reshape(head_shape)
    values_low = (slot_of(projected, 2) + value_bias).astype(jnp.bfloat16).reshape(head_shape)
    scaled = (
        jnp.einsum("bqhd,bkhd->bhqk", queries, keys_low, preferred_element_type=jnp.float32) * scale
    )
    row_top = jnp.max(scaled, axis=-1, keepdims=True)
    expos = jnp.exp(scaled - row_top)
    probs = expos / jnp.sum(expos, axis=-1, keepdims=True)
    probs_low = probs.astype(jnp.bfloat16)
    mixed = jnp.einsum("bhqk,bkhd->bhqd", probs_low, values_low, preferred_element_type=jnp.float32)
    mixed = mixed.astype(jnp.bfloat16)
    none = jnp.zeros_like(mixed)
    mixed_slots = interleave(none, none, none, mixed)
    middle = inputs + (times_transposed(mixed_slots, attn) + out_bias)
    normed2_f, norm2_back = jax.vjp(layer_norm, middle, ln2_gain, ln2_bias)
    normed2 = normed2_f.astype(jnp.bfloat16)
    upper = matmul(normed2, up) + up_bias
    hidden_f, gelu_back = jax.vjp(gelu_exact, upper)
    hidden = hidden_f.astype(jnp.bfloat16)
    output = middle + (times_transposed(hidden, down) + down_bias)
    activations = output.astype(jnp.bfloat16)
    grad_out = cotangent.astype(jnp.float32)
    grad_branch2 = cotangent
    down_bias_part = column_sums(grad_branch2)
    down_part = contract_rows(grad_branch2, hidden).astype(jnp.bfloat16)
    grad_upper = gelu_back(matmul(grad_branch2, down))[0].astype(jnp.bfloat16)
    up_bias_part = column_sums(grad_upper)
    up_part = contract_rows(normed2, grad_upper).astype(jnp.bfloat16)
    grad_normed2 = times_transposed(grad_upper, up)
    grad_mid_norm, ln2_gain_part, ln2_bias_part = norm2_back(grad_normed2)
    grad_middle = grad_out + grad_mid_norm
    grad_branch = grad_middle.astype(jnp.bfloat16)
    out_bias_part = column_sums(grad_branch)
    grad_mixed = slot_of(matmul(grad_branch, attn), 3).astype(jnp.bfloat16).reshape(head_shape)
    grad_probs = jnp.einsum(
        "bqhd,bkhd->bhqk", grad_mixed, values_low, preferred_element_type=jnp.float32
    )
    grad_values = jnp.einsum(
        "bhqk,bqhd->bhkd", probs_low, grad_mixed, preferred_element_type=jnp.float32
    )
    grad_values = grad_values.astype(jnp.bfloat16)
    inner = jnp.sum(probs * grad_probs, axis=-1, keepdims=True)
    grad_scores = (probs * (grad_probs - inner) * scale).astype(jnp.bfloat16)
    grad_queries = jnp.einsum(
        "bhqk,bkhd->bhqd", grad_scores, keys_low, preferred_element_type=jnp.float32
    )
    grad_queries = grad_queries.astype(jnp.bfloat16)
    grad_keys = jnp.einsum(
        "bhqk,bqhd->bhkd", grad_scores, queries, preferred_element_type=jnp.float32
    )
    grad_keys = grad_keys.astype(jnp.bfloat16)
    query_bias_part = jnp.sum(grad_queries.astype(jnp.float32), axis=(0, 2)).reshape(-1)
    value_bias_part = jnp.sum(grad_values.astype(jnp.float32), axis=(0, 2)).reshape(-1)
    grad_slots = interleave(grad_queries, grad_keys, grad_values, none)
    attn_part = contract_rows(
        jnp.concatenate([normed, grad_branch], axis=0),
        jnp.concatenate([grad_slots, mixed_slots], axis=0),
    ).astype(jnp.bfloat16)
    grad_normed = times_transposed(grad_slots, attn)
    grad_in_norm, ln1_gain_part, ln1_bias_part = norm1_back(grad_normed)
    input_grad = grad_middle + grad_in_norm
    vectors = jnp.concatenate(
        [
            ln1_gain_part,
            ln1_bias_part,
            out_bias_part,
            ln2_gain_part,
            ln2_bias_part,
            down_bias_part,
            query_bias_part,
            value_bias_part,
            up_bias_part,
        ]
    ).reshape(-1, width)
    sums, vector_sums = reduce_gradients(
        [part.reshape(n_dp, rows, -1) for part in (down_part, up_part, attn_part)],
        vectors,
        n_dp,
        n_mp,
    )
    at = lax.axis_index("mp")
    up_width = w_up.shape[1]
    own_up = lax.dynamic_slice_in_dim(vector_sums[8:].reshape(-1), at * up_width, up_width)
    return (
        activations,
        input_grad,
        vector_sums[0],
        vector_sums[1],
        sums[2, :, :local],
        lax.dynamic_slice_in_dim(vector_sums[6], at * local, local),
        sums[2, :, local : 2 * local],
        sums[2, :, 2 * local : 3 * local],
        lax.dynamic_slice_in_dim(vector_sums[7], at * local, local),
        sums[2, :, 3 * local :],
        vector_sums[2],
        vector_sums[3],
        vector_sums[4],
        sums[1],
        own_up,
        sums[0],
        vector_sums[5],
    )


def solution(mesh):
    whole, rows, block, ends = P(), P(("dp", "mp"), None), P("dp", "mp"), P("mp")
    in_specs = (
        rows, rows, whole, whole, block, ends, block, block, ends, block,
        whole, whole, whole, block, ends, block, whole,
    )
    out_specs = (
        rows, rows, whole, whole, block, ends, block, block, ends, block,
        whole, whole, whole, block, ends, block, whole,
    )
    return jax.shard_map(
        functools.partial(per_device, mesh.shape["dp"], mesh.shape["mp"]),
        mesh=mesh,
        in_specs=in_specs,
        out_specs=out_specs,
        check_vma=False,
    )
```

```python
import functools

import jax
import jax.numpy as jnp
from jax import lax
from jax.experimental import pallas as pl
from jax.experimental.pallas import tpu as pltpu
from jax.sharding import PartitionSpec as P

HEAD_DIM = 64
SEQ = 197
MESH = pl.DeviceIdType.MESH

norm_eps = 1e-06


def layer_norm(inputs, gain, shift):
    row_mean = jnp.mean(inputs, axis=-1, keepdims=True)
    centred = inputs - row_mean
    variance = jnp.mean(centred * centred, axis=-1, keepdims=True)
    return centred * lax.rsqrt(variance + norm_eps) * gain + shift


def gelu_exact(upper):
    return jax.nn.gelu(upper, approximate=False)


def matmul(left, right):
    return jnp.dot(left, right, preferred_element_type=jnp.float32)


def contract_rows(left, right):
    return lax.dot_general(
        left, right, (((0,), (0,)), ((), ())), preferred_element_type=jnp.float32
    )


def times_transposed(left, right):
    return lax.dot_general(
        left, right, (((1,), (1,)), ((), ())), preferred_element_type=jnp.float32
    )


def column_sums(grads_low):
    return jnp.sum(grads_low.astype(jnp.float32), axis=0)


def flip(index, bit):
    return index + (1 << bit) * (1 - 2 * bit_of(index, bit))


def bit_of(index, bit):
    return lax.rem(lax.div(index, 1 << bit), 2)


def bits_in(size):
    return size.bit_length() - 1


def dp_order(n_bits, variant):
    rest = list(range(1, n_bits))
    if variant:
        rest = rest[::-1]
    return [0] + rest if n_bits else []


def greet(dp, mp, dp_bits, mp_bits):
    barrier = pltpu.get_barrier_semaphore()
    for bit in range(dp_bits):
        pl.semaphore_signal(barrier, inc=1, device_id=(flip(dp, bit), mp), device_id_type=MESH)
    for bit in range(mp_bits):
        pl.semaphore_signal(barrier, inc=1, device_id=(dp, flip(mp, bit)), device_id_type=MESH)
    pl.semaphore_wait(barrier, dp_bits + mp_bits)


def gather_plan(dp_bits, mp_bits, variant):
    stages = []
    done_mp = []
    for bit in range(mp_bits)[::-1]:
        stages.append(("mp", bit, (), tuple(done_mp)))
        done_mp.append(bit)
    done_dp = []
    for bit in dp_order(dp_bits, variant)[::-1]:
        stages.append(("dp", bit, tuple(done_dp), tuple(done_mp)))
        done_dp.append(bit)
    return stages


def subsets(index, handled):
    out = [index]
    for bit in handled:
        out = out + [flip(item, bit) for item in out]
    return out


def gather_kernel(n_dp, n_mp, halves, n_mats, *refs):
    shards, bias = refs[:n_mats], refs[n_mats]
    outs, bias_all = refs[n_mats + 1 : 2 * n_mats + 1], refs[2 * n_mats + 1]
    send_sem, recv_sem, own_sem, bias_send, bias_recv = refs[2 * n_mats + 2 :]
    dp_bits, mp_bits = bits_in(n_dp), bits_in(n_mp)
    rows, width = shards[0].shape
    piece = rows // halves
    dp, mp = lax.axis_index("dp"), lax.axis_index("mp")

    def columns(m):
        return pl.ds(pl.multiple_of(m * width, width), width)

    def part(mat, half, d, m):
        row = pl.ds(half * piece, piece)
        if m is None:
            return outs[mat].at[d, row, :]
        return outs[mat].at[d, row, columns(m)]

    locals_ = []
    for mat in range(n_mats):
        copy = pltpu.make_async_copy(
            shards[mat], outs[mat].at[dp, :, columns(mp)], own_sem.at[mat]
        )
        copy.start()
        locals_.append(copy)
    greet(dp, mp, dp_bits, mp_bits)
    for copy in locals_:
        copy.wait()

    sent = []
    waiting = {}
    n_stages = dp_bits + mp_bits
    bias_all[mp] = bias[...]
    bias_wait = []

    def bias_run(stage):
        _, bit, _, done_mp = gather_plan(dp_bits, mp_bits, 0)[stage]
        slot = (1 << stage) - 1
        for number, (m, their_m) in enumerate(
            zip(subsets(mp, done_mp), subsets(flip(mp, bit), done_mp))
        ):
            sems = dict(
                send_sem=bias_send.at[slot + number],
                recv_sem=bias_recv.at[slot + number],
                device_id=(dp, flip(mp, bit)),
                device_id_type=MESH,
            )
            copy = pltpu.make_async_remote_copy(
                src_ref=bias_all.at[m], dst_ref=bias_all.at[m], **sems
            )
            copy.start()
            sent.append(copy)
            bias_wait.append(
                pltpu.make_async_remote_copy(
                    src_ref=bias_all.at[their_m], dst_ref=bias_all.at[their_m], **sems
                )
            )

    def run(mat, half, stage):
        variant = half if halves > 1 else mat % 2
        chunk = mat * halves + half
        axis, bit, done_dp, done_mp = gather_plan(dp_bits, mp_bits, variant)[stage]
        if axis == "mp":
            mine = [(dp, m) for m in subsets(mp, done_mp)]
            theirs = [(dp, m) for m in subsets(flip(mp, bit), done_mp)]
            target = (dp, flip(mp, bit))
        else:
            mine = [(d, None) for d in subsets(dp, done_dp)]
            theirs = [(d, None) for d in subsets(flip(dp, bit), done_dp)]
            target = (flip(dp, bit), mp)
        slot = 0
        for earlier in range(stage):
            _, _, e_dp, e_mp = gather_plan(dp_bits, mp_bits, variant)[earlier]
            slot += 1 << (len(e_mp) if earlier < mp_bits else len(e_dp))
        for number, ((d, m), (their_d, their_m)) in enumerate(zip(mine, theirs)):
            sems = dict(
                send_sem=send_sem.at[chunk, slot + number],
                recv_sem=recv_sem.at[chunk, slot + number],
                device_id=target,
                device_id_type=MESH,
            )
            source = part(mat, half, d, m)
            copy = pltpu.make_async_remote_copy(src_ref=source, dst_ref=source, **sems)
            copy.start()
            sent.append(copy)
            landing = part(mat, half, their_d, their_m)
            waiting.setdefault((mat, half), []).append(
                pltpu.make_async_remote_copy(src_ref=landing, dst_ref=landing, **sems)
            )

    def settle(mat, half):
        for copy in waiting.pop((mat, half), []):
            copy.wait_recv()

    for step in range(n_mats + n_stages):
        if step <= mp_bits:
            while bias_wait:
                bias_wait.pop().wait_recv()
            if step < mp_bits:
                bias_run(step)
        for stage in range(n_stages + 1)[::-1]:
            mat = step - stage
            if 0 <= mat < n_mats:
                for half in range(halves):
                    settle(mat, half)
                    if stage < n_stages:
                        run(mat, half, stage)
    for copy in sent:
        copy.wait_send()


def gather_weights(shards, bias, n_dp, n_mp):
    rows, width = shards[0].shape
    n_mats = len(shards)
    halves = 2 if rows % 32 == 0 else 1
    copies = (n_mp - 1) + (n_dp - 1)
    return pl.pallas_call(
        functools.partial(gather_kernel, n_dp, n_mp, halves, n_mats),
        out_shape=[jax.ShapeDtypeStruct((n_dp, rows, n_mp * width), jnp.bfloat16)] * n_mats
        + [jax.ShapeDtypeStruct((n_mp,) + bias.shape, jnp.float32)],
        in_specs=[pl.BlockSpec(memory_space=pl.ANY)] * n_mats
        + [pl.BlockSpec(memory_space=pltpu.VMEM)],
        out_specs=[pl.BlockSpec(memory_space=pl.ANY)] * n_mats
        + [pl.BlockSpec(memory_space=pltpu.VMEM)],
        scratch_shapes=[
            pltpu.SemaphoreType.DMA((n_mats * halves, copies)),
            pltpu.SemaphoreType.DMA((n_mats * halves, copies)),
            pltpu.SemaphoreType.DMA((n_mats,)),
            pltpu.SemaphoreType.DMA((max(n_mp - 1, 1),)),
            pltpu.SemaphoreType.DMA((max(n_mp - 1, 1),)),
        ],
        compiler_params=pltpu.CompilerParams(collective_id=0, has_side_effects=True),
    )(*shards, bias)


def reduce_kernel(n_dp, n_mp, halves, n_mats, *refs):
    parts, vectors = refs[:n_mats], refs[n_mats]
    sums, vector_sum = refs[n_mats + 1 : n_mats + 3]
    dp_bits, mp_bits = bits_in(n_dp), bits_in(n_mp)
    n_stages = dp_bits + mp_bits
    scratch = refs[n_mats + 3 :]
    kept = scratch[0]
    landed = scratch[1 : 1 + n_stages]
    vector_in = scratch[1 + n_stages]
    vector_at = scratch[2 + n_stages]
    send_sem, recv_sem, kept_sem, v_send, v_recv = scratch[3 + n_stages :]
    rows = sums.shape[1]
    width = sums.shape[2]
    piece = rows // halves
    group = 16 if piece % 16 == 0 else piece
    dp, mp = lax.axis_index("dp"), lax.axis_index("mp")

    def arranged(order, fixed_bit, value):
        out = [value * (1 << fixed_bit)]
        for bit in order:
            out = [item + (side << bit) for item in out for side in (0, 1)]
        return out

    greet(dp, mp, dp_bits, mp_bits)
    vector_at[0] = vectors[...]
    sent = []
    waiting = {}
    vector_wait = []

    def partner(axis, bit):
        if axis == "dp":
            return (flip(dp, bit), mp)
        return (dp, flip(mp, bit))

    def stages_of(variant):
        order = dp_order(dp_bits, variant)
        return [("dp", bit) for bit in order] + [("mp", bit) for bit in range(mp_bits)]

    def send(key, source, landing, sem, target):
        copy = pltpu.make_async_remote_copy(
            src_ref=source,
            dst_ref=landing,
            send_sem=send_sem.at[sem],
            recv_sem=recv_sem.at[sem],
            device_id=target,
            device_id_type=MESH,
        )
        copy.start()
        sent.append(copy)
        waiting.setdefault(key, []).append(copy)

    first = n_dp // 2

    def run(mat, half, stage):
        variant = half if halves > 1 else mat % 2
        chunk = mat * halves + half
        plan = stages_of(variant)
        axis, bit = plan[stage]
        target = partner(axis, bit)
        key = (mat, half)
        row = pl.ds(half * piece, piece)
        if stage == 0:
            order = [b for _, b in plan[1:dp_bits]]
            side = bit_of(dp, bit)
            for number, block in enumerate(arranged(order, bit, 1 - side)):
                send(
                    key,
                    parts[mat].at[block, row, :],
                    landed[0].at[chunk, number],
                    (chunk, number),
                    target,
                )
            for number, block in enumerate(arranged(order, bit, side)):
                copy = pltpu.make_async_copy(
                    parts[mat].at[block, row, :], kept.at[chunk, number], kept_sem.at[chunk, number]
                )
                copy.start()
                waiting[key].append(copy)
        elif axis == "dp":
            count = n_dp >> (stage + 1)
            start = (1 - bit_of(dp, bit)) * count
            send(
                key,
                landed[stage - 1].at[chunk, pl.ds(start, count)],
                landed[stage].at[chunk],
                (chunk, first + stage - 1),
                target,
            )
        else:
            count = n_mp >> (bit + 1)
            slot = first + dp_bits - 1 + (n_mp - (n_mp >> bit))
            for number in range(count):
                block = 2 * number + 1 - bit_of(mp, bit)
                send(
                    key,
                    landed[stage - 1].at[chunk, 0, :, pl.ds(pl.multiple_of(block * width, width), width)],
                    landed[stage].at[chunk, 0, :, pl.ds(number * width, width)],
                    (chunk, slot + number),
                    target,
                )

    def settle(mat, half, stage):
        variant = half if halves > 1 else mat % 2
        chunk = mat * halves + half
        for copy in waiting.pop((mat, half)):
            if hasattr(copy, "wait_recv") and copy.is_remote:
                copy.wait_recv()
            else:
                copy.wait()
        axis, bit = stages_of(variant)[stage]
        last = stage == n_stages - 1
        into = landed[stage]
        blocks = into.shape[1]

        @pl.loop(0, blocks * (piece // group))
        def _(at):
            block = lax.div(at, piece // group)
            start = lax.rem(at, piece // group) * group
            if group % 16 == 0:
                start = pl.multiple_of(start, group)
            here = pl.ds(start, group)
            if axis == "dp":
                if stage == 0:
                    own = kept[chunk, block, here, :]
                else:
                    base = bit_of(dp, bit) * blocks
                    own = landed[stage - 1][chunk, base + block, here, :]
                total = own.astype(jnp.float32) + into[chunk, block, here, :].astype(jnp.float32)
                into[chunk, block, here, :] = total.astype(jnp.bfloat16)
            else:
                for number in range(n_mp >> (bit + 1)):
                    source = 2 * number + bit_of(mp, bit)
                    own = landed[stage - 1][
                        chunk, 0, here, pl.ds(pl.multiple_of(source * width, width), width)
                    ]
                    cols = pl.ds(number * width, width)
                    total = own.astype(jnp.float32) + into[chunk, 0, here, cols].astype(jnp.float32)
                    if last:
                        place = pl.ds(half * piece + start, group)
                        sums[mat, place, :] = total
                    else:
                        into[chunk, 0, here, cols] = total.astype(jnp.bfloat16)

    vector_plan = stages_of(0)

    def vector_send(stage):
        axis, bit = vector_plan[stage]
        copy = pltpu.make_async_remote_copy(
            src_ref=vector_at.at[stage],
            dst_ref=vector_in.at[stage],
            send_sem=v_send.at[stage],
            recv_sem=v_recv.at[stage],
            device_id=partner(axis, bit),
            device_id_type=MESH,
        )
        copy.start()
        vector_wait.append(copy)

    def vector_settle(stage):
        vector_wait[stage].wait()
        total = vector_at[stage] + vector_in[stage]
        if stage == n_stages - 1:
            vector_sum[...] = total
        else:
            vector_at[stage + 1] = total

    for step in range(n_mats + n_stages):
        if 1 <= step <= n_stages:
            vector_settle(step - 1)
        if step < n_stages:
            vector_send(step)
        for stage in range(n_stages + 1)[::-1]:
            mat = step - stage
            if 0 <= mat < n_mats:
                for half in range(halves):
                    if stage > 0:
                        settle(mat, half, stage - 1)
                    if stage < n_stages:
                        run(mat, half, stage)
    for copy in sent:
        copy.wait_send()


def reduce_gradients(parts, vectors, n_dp, n_mp):
    n_mats = len(parts)
    _, rows, full = parts[0].shape
    width = full // n_mp
    halves = 2 if rows % 32 == 0 else 1
    piece = rows // halves
    chunks = n_mats * halves
    dp_bits, mp_bits = bits_in(n_dp), bits_in(n_mp)
    n_stages = dp_bits + mp_bits
    landings = [
        pltpu.VMEM((chunks, n_dp >> (stage + 1), piece, full), jnp.bfloat16)
        for stage in range(dp_bits)
    ] + [
        pltpu.VMEM((chunks, 1, piece, full >> (stage + 1)), jnp.bfloat16)
        for stage in range(mp_bits)
    ]
    copies = n_dp // 2 + dp_bits - 1 + n_mp - 1
    return pl.pallas_call(
        functools.partial(reduce_kernel, n_dp, n_mp, halves, n_mats),
        out_shape=[
            jax.ShapeDtypeStruct((n_mats, rows, width), jnp.float32),
            jax.ShapeDtypeStruct(vectors.shape, jnp.float32),
        ],
        in_specs=[pl.BlockSpec(memory_space=pl.ANY)] * n_mats
        + [pl.BlockSpec(memory_space=pltpu.VMEM)],
        out_specs=[pl.BlockSpec(memory_space=pltpu.VMEM)] * 2,
        scratch_shapes=[
            pltpu.VMEM((chunks, n_dp // 2, piece, full), jnp.bfloat16),
            *landings,
            pltpu.VMEM((n_stages,) + vectors.shape, jnp.float32),
            pltpu.VMEM((n_stages,) + vectors.shape, jnp.float32),
            pltpu.SemaphoreType.DMA((chunks, copies)),
            pltpu.SemaphoreType.DMA((chunks, copies)),
            pltpu.SemaphoreType.DMA((chunks, n_dp // 2)),
            pltpu.SemaphoreType.DMA((n_stages,)),
            pltpu.SemaphoreType.DMA((n_stages,)),
        ],
        compiler_params=pltpu.CompilerParams(
            collective_id=1, has_side_effects=True, vmem_limit_bytes=48 * 1024 * 1024
        ),
    )(*parts, vectors)


def per_device(
    n_dp,
    n_mp,
    tokens,
    cotangent,
    ln1_gain,
    ln1_bias,
    w_query,
    query_bias,
    w_key,
    w_value,
    value_bias,
    w_out,
    out_bias,
    ln2_gain,
    ln2_bias,
    w_up,
    up_bias,
    w_down,
    down_bias,
):
    own_rows, width = tokens.shape
    images = own_rows // SEQ
    rows, local = w_query.shape
    heads = width // HEAD_DIM
    scale = HEAD_DIM ** (-0.5)
    head_shape = (images, heads, SEQ, HEAD_DIM)
    attn_shard = jnp.concatenate([w_query, w_key, w_value, w_out], axis=1)
    bias = jnp.concatenate([query_bias, value_bias, up_bias])
    *weights, both = gather_weights((attn_shard, w_up, w_down), bias.reshape(-1, 128), n_dp, n_mp)
    attn, up, down = (full.reshape(n_dp * rows, -1) for full in weights)
    both = both.reshape(n_mp, -1)
    query_bias = both[:, :local].reshape(-1)
    value_bias = both[:, local : 2 * local].reshape(-1)
    up_bias = both[:, 2 * local :].reshape(-1)

    near = local // HEAD_DIM

    def interleave(*slots):
        stacked = jnp.stack(
            [s.reshape(images, n_mp, near, SEQ, HEAD_DIM) for s in slots], axis=2
        )
        return stacked.transpose(0, 4, 1, 2, 3, 5).reshape(own_rows, -1)

    def head_major(array):
        array = lax.optimization_barrier(array)
        return array.reshape(images, SEQ, n_mp, 4, near, HEAD_DIM).transpose(0, 2, 3, 4, 1, 5)

    inputs = tokens.astype(jnp.float32)
    normed_f, norm1_back = jax.vjp(layer_norm, inputs, ln1_gain, ln1_bias)
    normed = normed_f.astype(jnp.bfloat16)
    zero_bias = jnp.zeros((n_mp, local), jnp.float32)
    slot_bias = jnp.stack(
        [query_bias.reshape(n_mp, local), zero_bias, value_bias.reshape(n_mp, local), zero_bias],
        axis=1,
    ).reshape(-1)
    projected = head_major((matmul(normed, attn) + slot_bias).astype(jnp.bfloat16))
    queries, keys_low, values_low = (projected[:, :, slot].reshape(head_shape) for slot in range(3))
    scaled = (
        jnp.einsum("bhqd,bhkd->bhqk", queries, keys_low, preferred_element_type=jnp.float32) * scale
    )
    row_top = jnp.max(scaled, axis=-1, keepdims=True)
    expos = jnp.exp(scaled - row_top)
    probs = expos / jnp.sum(expos, axis=-1, keepdims=True)
    probs_low = probs.astype(jnp.bfloat16)
    mixed = jnp.einsum("bhqk,bhkd->bhqd", probs_low, values_low, preferred_element_type=jnp.float32)
    mixed = mixed.astype(jnp.bfloat16)
    none = jnp.zeros_like(mixed)
    mixed_slots = interleave(none, none, none, mixed)
    middle = inputs + (times_transposed(mixed_slots, attn) + out_bias)
    normed2_f, norm2_back = jax.vjp(layer_norm, middle, ln2_gain, ln2_bias)
    normed2 = normed2_f.astype(jnp.bfloat16)
    upper = matmul(normed2, up) + up_bias
    hidden_f, gelu_back = jax.vjp(gelu_exact, upper)
    hidden = hidden_f.astype(jnp.bfloat16)
    output = middle + (times_transposed(hidden, down) + down_bias)
    activations = output.astype(jnp.bfloat16)
    grad_out = cotangent.astype(jnp.float32)
    grad_branch2 = cotangent
    down_bias_part = column_sums(grad_branch2)
    down_part = contract_rows(grad_branch2, hidden).astype(jnp.bfloat16)
    grad_upper = gelu_back(matmul(grad_branch2, down))[0].astype(jnp.bfloat16)
    up_bias_part = column_sums(grad_upper)
    up_part = contract_rows(normed2, grad_upper).astype(jnp.bfloat16)
    grad_normed2 = times_transposed(grad_upper, up)
    grad_mid_norm, ln2_gain_part, ln2_bias_part = norm2_back(grad_normed2)
    grad_middle = grad_out + grad_mid_norm
    grad_branch = grad_middle.astype(jnp.bfloat16)
    out_bias_part = column_sums(grad_branch)
    grad_mixed = head_major(matmul(grad_branch, attn).astype(jnp.bfloat16))[:, :, 3].reshape(head_shape)
    grad_probs = jnp.einsum(
        "bhqd,bhkd->bhqk", grad_mixed, values_low, preferred_element_type=jnp.float32
    )
    grad_values = jnp.einsum(
        "bhqk,bhqd->bhkd", probs_low, grad_mixed, preferred_element_type=jnp.float32
    )
    grad_values = grad_values.astype(jnp.bfloat16)
    inner = jnp.sum(probs * grad_probs, axis=-1, keepdims=True)
    grad_scores = (probs * (grad_probs - inner) * scale).astype(jnp.bfloat16)
    grad_queries = jnp.einsum(
        "bhqk,bhkd->bhqd", grad_scores, keys_low, preferred_element_type=jnp.float32
    )
    grad_queries = grad_queries.astype(jnp.bfloat16)
    grad_keys = jnp.einsum(
        "bhqk,bhqd->bhkd", grad_scores, queries, preferred_element_type=jnp.float32
    )
    grad_keys = grad_keys.astype(jnp.bfloat16)
    query_bias_part = jnp.sum(grad_queries.astype(jnp.float32), axis=(0, 2)).reshape(-1)
    value_bias_part = jnp.sum(grad_values.astype(jnp.float32), axis=(0, 2)).reshape(-1)
    grad_slots = interleave(grad_queries, grad_keys, grad_values, none)
    attn_part = contract_rows(
        jnp.concatenate([normed, grad_branch], axis=0),
        jnp.concatenate([grad_slots, mixed_slots], axis=0),
    ).astype(jnp.bfloat16)
    grad_normed = times_transposed(grad_slots, attn)
    grad_in_norm, ln1_gain_part, ln1_bias_part = norm1_back(grad_normed)
    input_grad = grad_middle + grad_in_norm
    vectors = jnp.concatenate(
        [
            ln1_gain_part,
            ln1_bias_part,
            out_bias_part,
            ln2_gain_part,
            ln2_bias_part,
            down_bias_part,
            query_bias_part,
            value_bias_part,
            up_bias_part,
        ]
    ).reshape(-1, width)
    sums, vector_sums = reduce_gradients(
        [part.reshape(n_dp, rows, -1) for part in (down_part, up_part, attn_part)],
        vectors,
        n_dp,
        n_mp,
    )
    at = lax.axis_index("mp")
    up_width = w_up.shape[1]
    own_up = lax.dynamic_slice_in_dim(vector_sums[8:].reshape(-1), at * up_width, up_width)
    return (
        activations,
        input_grad,
        vector_sums[0],
        vector_sums[1],
        sums[2, :, :local],
        lax.dynamic_slice_in_dim(vector_sums[6], at * local, local),
        sums[2, :, local : 2 * local],
        sums[2, :, 2 * local : 3 * local],
        lax.dynamic_slice_in_dim(vector_sums[7], at * local, local),
        sums[2, :, 3 * local :],
        vector_sums[2],
        vector_sums[3],
        vector_sums[4],
        sums[1],
        own_up,
        sums[0],
        vector_sums[5],
    )


def solution(mesh):
    whole, rows, block, ends = P(), P(("dp", "mp"), None), P("dp", "mp"), P("mp")
    in_specs = (
        rows, rows, whole, whole, block, ends, block, block, ends, block,
        whole, whole, whole, block, ends, block, whole,
    )
    out_specs = (
        rows, rows, whole, whole, block, ends, block, block, ends, block,
        whole, whole, whole, block, ends, block, whole,
    )
    return jax.shard_map(
        functools.partial(per_device, mesh.shape["dp"], mesh.shape["mp"]),
        mesh=mesh,
        in_specs=in_specs,
        out_specs=out_specs,
        check_vma=False,
    )
```
